32 devices in a mesh: groups: 2 (over y), seq: 4 (over z), chan: 4 (over x, core).
Axes of the slice: x: 2, y: 2, z: 4, core: 2. Of those that a mesh axis runs over, the one named last changes fastest.
Arguments:
- se_qkv: bfloat16 [3, 2560, 8192], P(None, ('groups', 'seq'), 'chan'), parts along dimension 1, may hold values from -6 to 6
- se_short: float32 [3, 3, 8192], P(None, None, 'chan'), may hold values from -3.5 to 3.5
- se_filter: float32 [7, 8192], P(None, 'chan'), may hold values from -2 to 2
- mr_qkv: bfloat16 [3, 2560, 8192], P(None, ('groups', 'seq'), 'chan'), parts along dimension 1, may hold values from -6 to 6
- mr_short: float32 [3, 3, 8192], P(None, None, 'chan'), may hold values from -3.5 to 3.5
- mr_filter: float32 [128, 8192], P(None, 'chan'), may hold values from -1 to 1
- mr_decay: float32 [8192], P('chan'), may hold values from 0.004 to 0.1
- attn_qkv: bfloat16 [3, 2560, 8192], P(None, ('groups', 'seq'), 'chan'), parts along dimension 1, may hold values from -140 to 140, as said below
Outputs:
- se_out: bfloat16 [2560, 8192], P(('groups', 'seq'), 'chan'), parts along dimension 0
- mr_out: bfloat16 [2560, 8192], P(('groups', 'seq'), 'chan'), parts along dimension 0
- attn_out: bfloat16 [2560, 8192], P(('groups', 'seq'), 'chan'), parts along dimension 0
The draws below stay inside these ranges and needn't reach their ends.
There are 2 independent parts, one for each index of `groups`. The reference program is written for one: setup_inputs(seed, part) draws one part's arguments, and reference() takes and returns one part's arrays. A program takes and returns all parts, laid end to end along the dimension named above; an argument that names none is the same for every part. Nothing has to cross between parts.
Inputs may be any that keep to these rules, and one draw needn't show every extreme that they name: `attn_qkv`: Queries, keys and values of attention as bfloat16 numbers of order one; some queries may be large.
All inputs are finite; a program needn't handle non-finite values.
Results may differ from the reference program's by a relative error of at most 0.0035.
Values may be sent and summed in bfloat16 or wider, within the bound.
No kernel may reach another device: no remote copies, remote signals or barrier semaphores. Data moves between devices by JAX's collectives and lax.ppermute only.
A program may use at most 128 MiB of HBM per device.

```python
import math
import jax
import jax.numpy as jnp
from jax import lax

HD = 128
D = 8192
KSHORT = 3
KSE = 7
KMR = 128
LENGTH = 1280


def draw_attn_qkv(key, part):
    streams = jax.random.split(key, 3)
    query = 1.3 * jax.random.truncated_normal(streams[0], -6.0, 6.0, (LENGTH, D), jnp.float32)
    keyrows = 1.3 * jax.random.truncated_normal(streams[1], -6.0, 6.0, (LENGTH, D), jnp.float32)
    valrows = 4.0 * jax.random.truncated_normal(streams[2], -6.0, 6.0, (LENGTH, D), jnp.float32)
    return jnp.stack([query, keyrows, valrows]).astype(jnp.bfloat16)


def steps_of(stream_key, extent, shards, smallest, top_value):
    def one(dim, shards_of):
        draws = jax.random.uniform(jax.random.fold_in(jax.random.fold_in(stream_key, 6), dim), (shards_of,), jnp.float32, smallest / len(shards), top_value / len(shards))
        return jnp.repeat(jnp.exp(draws), extent[dim] // shards_of).reshape((-1,) + (1,) * (len(extent) - dim - 1))

    gain = one(*shards[0])
    for cut in shards[1:]:
        gain = gain * one(*cut)
    return gain


def bell_draw(stream_key, dims, width, limit, pieces=(), kind=jnp.bfloat16):
    values = jax.random.normal(stream_key, dims, jnp.float32) * width
    if len(pieces) > 0:
        values = steps_of(stream_key, dims, pieces, -0.22, 0.18) * values
    return jnp.clip(values, min=-limit, max=limit).astype(kind)


def setup_inputs(seed: int = 0, part: int = 0) -> dict:
    key_of = jax.random.split(jax.random.key(seed), 9)
    own_keys = jax.random.split(jax.random.fold_in(key_of[8], part), 9)
    return {
        "se_qkv": bell_draw(own_keys[0], (3, LENGTH, D), 1.0, 6.0, ((1, 4), (2, 4))),
        "se_short": bell_draw(key_of[1], (KSHORT, 3, D), KSHORT ** -0.5, 3.5, ((2, 4),), jnp.float32),
        "se_filter": bell_draw(key_of[2], (KSE, D), KSE ** -0.5, 2.0, ((1, 4),), jnp.float32),
        "mr_qkv": bell_draw(own_keys[3], (3, LENGTH, D), 1.0, 6.0, ((1, 4), (2, 4))),
        "mr_short": bell_draw(key_of[4], (KSHORT, 3, D), KSHORT ** -0.5, 3.5, ((2, 4),), jnp.float32),
        "mr_filter": bell_draw(key_of[5], (KMR, D), 32 ** -0.5, 1.0, ((1, 4),), jnp.float32),
        "mr_decay": jnp.clip(jnp.exp(math.log(0.1) - 3.218876 * jax.random.uniform(key_of[6], (D,), jnp.float32) ** steps_of(key_of[6], (D,), ((0, 4),), -0.2, 0.2)), 0.004, 0.1),
        "attn_qkv": draw_attn_qkv(jax.random.fold_in(jax.random.fold_in(key_of[8], part), 71), part),
    }


def causal_valid(extended, taps):
    count = taps.shape[0]
    out_len = extended.shape[0] - count + 1

    def add_tap(index, accum):
        piece = lax.dynamic_slice_in_dim(extended, index, out_len, 0)
        return accum + taps[count - 1 - index][None, :] * piece
    start = jnp.zeros((out_len, extended.shape[1]), extended.dtype)
    return lax.fori_loop(0, count, add_tap, start)

def hyena(qkv, short_taps, filter_taps):
    lead = short_taps.shape[0] - 1
    reach = filter_taps.shape[0] - 1
    query = jnp.pad(qkv[0].astype(jnp.float32), ((lead, 0), (0, 0)))
    keyrows = jnp.pad(qkv[1].astype(jnp.float32), ((lead + reach, 0), (0, 0)))
    valrows = jnp.pad(qkv[2].astype(jnp.float32), ((lead + reach, 0), (0, 0)))
    query_f = causal_valid(query, short_taps[:, 0])
    key_f = causal_valid(keyrows, short_taps[:, 1])
    val_f = causal_valid(valrows, short_taps[:, 2])
    return (query_f * causal_valid(key_f * val_f, filter_taps)).astype(jnp.bfloat16)

def one_head(operands):
    query, keyrows, valrows = operands
    length = query.shape[0]
    scores = jnp.dot(query, keyrows.T, preferred_element_type=jnp.float32) / jnp.sqrt(jnp.float32(HD))
    visible = jnp.arange(length)[None, :] <= jnp.arange(length)[:, None]
    scores = jnp.where(visible, scores, jnp.float32(-1e+30))
    peak = lax.optimization_barrier(jnp.max(scores, axis=1, keepdims=True))
    weights = jnp.where(visible, jnp.exp(scores - peak), jnp.float32(0.0))
    total = lax.optimization_barrier(jnp.sum(weights, axis=1, keepdims=True))
    mixed = jnp.dot(weights.astype(jnp.bfloat16), valrows, preferred_element_type=jnp.float32)
    return (mixed / total).astype(jnp.bfloat16)

def reference(se_qkv, se_short, se_filter, mr_qkv, mr_short, mr_filter, mr_decay, attn_qkv):
    se_out = hyena(se_qkv, se_short, se_filter)
    steps_idx = jnp.arange(mr_filter.shape[0]).astype(jnp.float32)
    mr_taps = mr_filter * jnp.exp(-mr_decay[None, :] * steps_idx[:, None])
    mr_out = hyena(mr_qkv, mr_short, mr_taps)
    length = attn_qkv.shape[1]
    heads = attn_qkv.shape[2] // HD
    split = attn_qkv.reshape(3, length, heads, HD).transpose(0, 2, 1, 3)
    result = lax.map(one_head, (split[0], split[1], split[2]))
    attn_out = result.transpose(1, 0, 2).reshape(length, heads * HD)
    return (se_out, mr_out, attn_out)
```

```python
import functools

import jax
import jax.numpy as jnp
import ml_dtypes
import numpy as np
from jax import lax
from jax.experimental import pallas as pl
from jax.experimental.pallas import tpu as pltpu
from jax.sharding import PartitionSpec as P

HD = 128
F32 = jnp.float32
BF16 = jnp.bfloat16
SCALE2 = float(np.log2(np.e) / np.sqrt(HD))
CHUNKS = (5, 5, 4, 2)
STAT_ROWS = 16
WINDOW = 256
BLOCK = 128
VMEM_LIMIT = 48 * 1024 * 1024


def split_np(value):
    high = value.astype(ml_dtypes.bfloat16)
    low = (value - high.astype(np.float64)).astype(ml_dtypes.bfloat16)
    return high, low


def transforms():
    bins = np.arange(WINDOW // 2)
    omega = 2.0 * np.pi * (bins + 0.5) / WINDOW
    place = np.arange(WINDOW)
    angle = omega[:, None] * place[None, :]
    forward = np.concatenate([np.cos(angle), -np.sin(angle)], axis=0)
    back = (2.0 / WINDOW) * np.concatenate(
        [np.cos(angle[:, BLOCK:]).T, -np.sin(angle[:, BLOCK:]).T], axis=1
    )
    f_high, f_low = split_np(forward)
    b_high, b_low = split_np(back)
    return np.concatenate([f_high, f_low], axis=0), np.concatenate([b_high, b_low], axis=0)


def halves(value):
    high = value.astype(BF16)
    return high, (value - high.astype(F32)).astype(BF16)


def dot(left, right):
    return jnp.dot(left, right, preferred_element_type=F32)


def forward_of(fwd, x_high):
    both = dot(fwd, x_high)
    return both[:WINDOW] + both[WINDOW:]


def spectral(u_spec, f_spec):
    half = WINDOW // 2
    ur, ui = u_spec[:half], u_spec[half:]
    fr, fi = f_spec[:half], f_spec[half:]
    return jnp.concatenate([ur * fr - ui * fi, ur * fi + ui * fr], axis=0)


def back_of(inv, y_spec):
    high, low = halves(y_spec)
    both = dot(inv, high)
    return both[:BLOCK] + both[BLOCK:] + dot(inv[:BLOCK], low)


def featurize(scratch, taps, first, count):
    return (
        taps[0] * scratch[first : first + count]
        + taps[1] * scratch[first - 1 : first - 1 + count]
        + taps[2] * scratch[first - 2 : first - 2 + count]
    )


def tap_rows(short_ref, which):
    return [short_ref[i, which : which + 1, :] for i in range(3)]


def se_kernel(qkv_ref, tail_ref, short_ref, filt_ref, out_ref, q_s, k_s, v_s, u_s):
    rows = qkv_ref.shape[1]
    width = qkv_ref.shape[2]
    tail = tail_ref[...].astype(F32)
    zero = jnp.zeros((8, width), F32)
    k_s[0:8] = zero
    v_s[0:8] = zero
    k_s[8:16] = tail[0:8]
    v_s[8:16] = tail[8:16]
    q_s[0:8] = jnp.concatenate([zero[:6], tail[16:18]], axis=0)
    q_s[8 : 8 + rows] = qkv_ref[0].astype(F32)
    k_s[16 : 16 + rows] = qkv_ref[1].astype(F32)
    v_s[16 : 16 + rows] = qkv_ref[2].astype(F32)
    tq, tk, tv = (tap_rows(short_ref, j) for j in range(3))
    taps = [filt_ref[i : i + 1, :] for i in range(filt_ref.shape[0])]
    u_s[0:8] = featurize(k_s, tk, 8, 8) * featurize(v_s, tv, 8, 8)
    step = 64
    for r in range(0, rows, step):
        u_s[8 + r : 8 + r + step] = featurize(k_s, tk, 16 + r, step) * featurize(
            v_s, tv, 16 + r, step
        )
    for r in range(0, rows, step):
        acc = taps[0] * u_s[8 + r : 8 + r + step]
        for i in range(1, len(taps)):
            acc = acc + taps[i] * u_s[8 + r - i : 8 + r - i + step]
        out_ref[r : r + step] = (featurize(q_s, tq, 8 + r, step) * acc).astype(BF16)


def mr_tail_kernel(k_ref, v_ref, short_ref, out_ref, k_s, v_s):
    half = k_ref.shape[1]
    k_s[...] = k_ref[0].astype(F32)
    v_s[...] = v_ref[0].astype(F32)
    tk, tv = tap_rows(short_ref, 1), tap_rows(short_ref, 2)
    first = half - BLOCK
    for r in range(0, BLOCK, 64):
        out_ref[r : r + 64] = (
            featurize(k_s, tk, first + r, 64) * featurize(v_s, tv, first + r, 64)
        ).astype(BF16)


def mr_main_kernel(
    qkv_ref, tail_ref, short_ref, filt_ref, decay_ref, fwd_ref, inv_ref,
    out_ref, spec_ref, lead_ref, q_s, k_s, v_s, u_s,
):
    rows = qkv_ref.shape[1]
    width = qkv_ref.shape[2]
    tail = tail_ref[...].astype(F32)
    zero = jnp.zeros((6, width), F32)
    q_s[0:8] = jnp.concatenate([zero, tail[18:20]], axis=0)
    k_s[0:8] = jnp.concatenate([zero, tail[20:22]], axis=0)
    v_s[0:8] = jnp.concatenate([zero, tail[22:24]], axis=0)
    q_s[8 : 8 + rows] = qkv_ref[0].astype(F32)
    k_s[8 : 8 + rows] = qkv_ref[1].astype(F32)
    v_s[8 : 8 + rows] = qkv_ref[2].astype(F32)
    tq, tk, tv = (tap_rows(short_ref, j) for j in range(3))
    step = 64
    for r in range(0, rows, step):
        u_s[r : r + step] = (
            featurize(k_s, tk, 8 + r, step) * featurize(v_s, tv, 8 + r, step)
        ).astype(BF16)
    lead_ref[...] = u_s[0:BLOCK]
    count = filt_ref.shape[0]
    place = lax.broadcasted_iota(jnp.int32, (count, 1), 0).astype(F32)
    taps = filt_ref[...] * jnp.exp(-decay_ref[...] * place)
    t_high, t_low = halves(taps)
    fwd = fwd_ref[...]
    inv = inv_ref[...]
    spec = forward_of(fwd[:, :count], t_high) + dot(fwd[:WINDOW, :count], t_low)
    spec_ref[...] = spec
    for start in range(BLOCK, rows, BLOCK):
        take = min(BLOCK, rows - start)
        window = BLOCK + take
        u_spec = forward_of(fwd[:, :window], u_s[start - BLOCK : start + take])
        mixed = back_of(inv, spectral(u_spec, spec))
        for r in range(0, take, step):
            out_ref[start + r : start + r + step] = (
                featurize(q_s, tq, 8 + start + r, step) * mixed[r : r + step]
            ).astype(BF16)


def mr_head_kernel(
    utail_ref, lead_ref, spec_ref, query_ref, tail_ref, short_ref, fwd_ref, inv_ref, part_ref,
    out_ref, q_s,
):
    del part_ref
    width = query_ref.shape[2]
    tail = tail_ref[...].astype(F32)
    q_s[0:8] = jnp.concatenate([jnp.zeros((6, width), F32), tail[18:20]], axis=0)
    q_s[8 : 8 + BLOCK] = query_ref[0].astype(F32)
    tq = tap_rows(short_ref, 0)
    window = jnp.concatenate([utail_ref[...], lead_ref[...]], axis=0)
    mixed = back_of(inv_ref[...], spectral(forward_of(fwd_ref[...], window), spec_ref[...]))
    for r in range(0, BLOCK, 64):
        out_ref[r : r + 64] = (featurize(q_s, tq, 8 + r, 64) * mixed[r : r + 64]).astype(BF16)


def nt_dot(left, right):
    return lax.dot_general(left, right, (((1,), (1,)), ((), ())), preferred_element_type=F32)


def tt_dot(left, right):
    return lax.dot_general(left, right, (((0,), (0,)), ((), ())), preferred_element_type=F32)


def partial_of(query, pairs, masked=False):
    scores = [nt_dot(keys, query) for keys, _ in pairs]
    if masked:
        shape = scores[0].shape
        below = lax.broadcasted_iota(jnp.int32, shape, 0) <= lax.broadcasted_iota(
            jnp.int32, shape, 1
        )
        scores = [jnp.where(below, scores[0], F32(-1e30))]
    peak = functools.reduce(jnp.maximum, [jnp.max(s, axis=0, keepdims=True) for s in scores])
    weights = [jnp.exp2((s - peak) * SCALE2) for s in scores]
    total = functools.reduce(jnp.add, [jnp.sum(w, axis=0, keepdims=True) for w in weights])
    mixed = functools.reduce(
        jnp.add, [tt_dot(vals, w.astype(BF16)) for w, (_, vals) in zip(weights, pairs)]
    )
    return mixed / total, peak * SCALE2 + jnp.log2(total)


def padded(rows):
    return -(-rows // 128) * 128


def pad_rows(value):
    extra = padded(value.shape[0]) - value.shape[0]
    if extra == 0:
        return value
    return jnp.concatenate([value, jnp.zeros((extra, value.shape[1]), value.dtype)], axis=0)


def stat_block(stat):
    high = stat.astype(BF16).astype(F32)
    mid = (stat - high).astype(BF16).astype(F32)
    low = (stat - high - mid).astype(BF16).astype(F32)
    lanes = stat.shape[1] // 128
    parts = [p[:, j * 128 : (j + 1) * 128] for p in (high, mid, low) for j in range(lanes)]
    parts.append(jnp.zeros((STAT_ROWS - len(parts), 128), F32))
    return jnp.concatenate(parts, axis=0).astype(BF16)


def stat_of(block, lanes):
    wide = block.astype(F32)
    total = wide[0:lanes] + wide[lanes : 2 * lanes] + wide[2 * lanes : 3 * lanes]
    return jnp.concatenate([total[j : j + 1] for j in range(lanes)], axis=1)


def put_payload(ref, mixed, stat, rows):
    ref[0, :rows] = mixed[:rows].astype(BF16)
    ref[0, rows : rows + STAT_ROWS] = stat_block(stat)


def local_kernel(q_ref, k_ref, v_ref, out_ref, stat_ref):
    rows = q_ref.shape[1]
    mixed, stat = partial_of(pad_rows(q_ref[0]), [(k_ref[0], v_ref[0])], masked=True)
    out_ref[0] = mixed.T[:rows]
    stat_ref[0] = jnp.broadcast_to(stat, stat_ref.shape[1:])


def cross_kernel(
    idx_ref, q_ref, k_ref, v_ref, first_ref, next_ref, last_ref, own_ref, up_ref, far_ref
):
    rows = q_ref.shape[1]
    index = idx_ref[0]

    @pl.when(index == 1)
    def _():
        early = (first_ref[0], first_ref[1])
        here = (k_ref[0], v_ref[0])
        both = jnp.concatenate([next_ref[...], last_ref[...]], axis=0)
        mixed, stat = partial_of(both, [early, here])
        mixed = mixed.T
        pad = jnp.zeros((1, padded(rows) - rows), F32)
        put_payload(up_ref, mixed[:rows], jnp.concatenate([stat[:, :rows], pad], axis=1), rows)
        put_payload(far_ref, mixed[rows:], jnp.concatenate([stat[:, rows:], pad], axis=1), rows)
        mixed, stat = partial_of(pad_rows(q_ref[0]), [early])
        put_payload(own_ref, mixed.T, stat, rows)

    @pl.when(index == 2)
    def _():
        mixed, stat = partial_of(pad_rows(next_ref[...]), [(k_ref[0], v_ref[0])])
        put_payload(up_ref, mixed.T, stat, rows)


def merge_kernel(idx_ref, loc_ref, stat_ref, own_ref, up_ref, far_ref, *rest):
    out_ref = rest[-1]
    rows = loc_ref.shape[1]
    lanes = padded(rows) // 128
    index = idx_ref[0]

    def merged(parts):
        stats = [stat_ref[0, 0:1]] + [stat_of(p[0, rows : rows + STAT_ROWS], lanes) for p in parts]
        values = [loc_ref[0]] + [p[0, :rows].astype(F32) for p in parts]
        top = functools.reduce(jnp.maximum, stats)
        weights = [jnp.exp2(s - top) for s in stats]
        total = functools.reduce(jnp.add, weights)
        result = 0.0
        for weight, value in zip(weights, values):
            column = jnp.broadcast_to(weight / total, (128, padded(rows))).T[:rows]
            result = result + column * value
        out_ref[...] = result.astype(BF16)

    @pl.when(index == 0)
    def _():
        out_ref[...] = loc_ref[0].astype(BF16)

    @pl.when(index == 1)
    def _():
        merged([own_ref])

    @pl.when(index == 2)
    def _():
        merged([up_ref])

    @pl.when(index == 3)
    def _():
        merged([up_ref, far_ref])


def params():
    return pltpu.CompilerParams(vmem_limit_bytes=VMEM_LIMIT)


def cost(flops, size):
    return pl.CostEstimate(flops=int(flops), bytes_accessed=int(size), transcendentals=0)


SMEM = pl.BlockSpec(memory_space=pltpu.SMEM)


def shape(dims, kind):
    return jax.ShapeDtypeStruct(dims, kind)


def full(array):
    return pl.BlockSpec(array.shape, lambda j: (0,) * array.ndim)


def se_mixer(qkv, tail, short, filt):
    rows, width = qkv.shape[1:]
    cols = 256
    return pl.pallas_call(
        se_kernel,
        grid=(width // cols,),
        in_specs=[
            pl.BlockSpec((3, rows, cols), lambda j: (0, 0, j)),
            pl.BlockSpec((tail.shape[0], cols), lambda j: (0, j)),
            pl.BlockSpec((3, 3, cols), lambda j: (0, 0, j)),
            pl.BlockSpec((filt.shape[0], cols), lambda j: (0, j)),
        ],
        out_specs=pl.BlockSpec((rows, cols), lambda j: (0, j)),
        out_shape=shape((rows, width), BF16),
        scratch_shapes=[
            pltpu.VMEM((8 + rows, cols), F32),
            pltpu.VMEM((16 + rows, cols), F32),
            pltpu.VMEM((16 + rows, cols), F32),
            pltpu.VMEM((8 + rows, cols), F32),
        ],
        compiler_params=params(),
        cost_estimate=cost(rows * width * 40, rows * width * 8),
        name="se_mixer",
    )(qkv, tail, short, filt)


def mr_tail(qkv, short):
    rows, width = qkv.shape[1:]
    cols = 512
    half = rows // 2
    return pl.pallas_call(
        mr_tail_kernel,
        grid=(width // cols,),
        in_specs=[
            pl.BlockSpec((1, half, cols), lambda j: (1, 1, j)),
            pl.BlockSpec((1, half, cols), lambda j: (2, 1, j)),
            pl.BlockSpec((3, 3, cols), lambda j: (0, 0, j)),
        ],
        out_specs=pl.BlockSpec((BLOCK, cols), lambda j: (0, j)),
        out_shape=shape((BLOCK, width), BF16),
        scratch_shapes=[pltpu.VMEM((half, cols), F32), pltpu.VMEM((half, cols), F32)],
        compiler_params=params(),
        cost_estimate=cost(BLOCK * width * 12, rows * width * 3),
        name="mr_tail",
    )(qkv, qkv, short)


def mr_main(qkv, tail, short, filt, decay, fwd, inv):
    rows, width = qkv.shape[1:]
    cols = 256
    col = lambda j: (0, j)
    return pl.pallas_call(
        mr_main_kernel,
        grid=(width // cols,),
        in_specs=[
            pl.BlockSpec((3, rows, cols), lambda j: (0, 0, j)),
            pl.BlockSpec((tail.shape[0], cols), col),
            pl.BlockSpec((3, 3, cols), lambda j: (0, 0, j)),
            pl.BlockSpec((filt.shape[0], cols), col),
            pl.BlockSpec((1, cols), col),
            full(fwd),
            full(inv),
        ],
        out_specs=[
            pl.BlockSpec((rows, cols), col),
            pl.BlockSpec((WINDOW, cols), col),
            pl.BlockSpec((BLOCK, cols), col),
        ],
        out_shape=[
            shape((rows, width), BF16),
            shape((WINDOW, width), F32),
            shape((BLOCK, width), BF16),
        ],
        scratch_shapes=[pltpu.VMEM((8 + rows, cols), F32)] * 3 + [pltpu.VMEM((rows, cols), BF16)],
        compiler_params=params(),
        cost_estimate=cost(WINDOW * WINDOW * width * 16, rows * width * 14),
        name="mr_main",
    )(qkv, tail, short, filt, decay[None, :], fwd, inv)


def mr_head(utail, lead, spec, qkv, tail, short, fwd, inv, part):
    rows, width = qkv.shape[1:]
    cols = 256
    col = lambda j: (0, j)
    return pl.pallas_call(
        mr_head_kernel,
        grid=(width // cols,),
        in_specs=[
            pl.BlockSpec((BLOCK, cols), col),
            pl.BlockSpec((BLOCK, cols), col),
            pl.BlockSpec((WINDOW, cols), col),
            pl.BlockSpec((1, BLOCK, cols), lambda j: (0, 0, j)),
            pl.BlockSpec((tail.shape[0], cols), col),
            pl.BlockSpec((3, 3, cols), lambda j: (0, 0, j)),
            full(fwd),
            full(inv),
            pl.BlockSpec(memory_space=pl.ANY),
        ],
        out_specs=pl.BlockSpec((BLOCK, cols), col),
        out_shape=shape((rows, width), BF16),
        scratch_shapes=[pltpu.VMEM((8 + BLOCK, cols), F32)],
        input_output_aliases={8: 0},
        compiler_params=params(),
        cost_estimate=cost(WINDOW * WINDOW * width * 6, rows * width * 4),
        name="mr_head",
    )(utail, lead, spec, qkv, tail, short, fwd, inv, part)


def head_spec(which, rows, offset):
    return pl.BlockSpec((1, rows, HD), lambda h: (which, 0, h + offset))


def local_attention(qkv):
    rows, width = qkv.shape[1:]
    heads = width // HD
    return pl.pallas_call(
        local_kernel,
        grid=(heads,),
        in_specs=[head_spec(j, rows, 0) for j in range(3)],
        out_specs=[
            pl.BlockSpec((1, rows, HD), lambda h: (h, 0, 0)),
            pl.BlockSpec((1, 8, padded(rows)), lambda h: (h, 0, 0)),
        ],
        out_shape=[shape((heads, rows, HD), F32), shape((heads, 8, padded(rows)), F32)],
        compiler_params=params(),
        cost_estimate=cost(heads * rows * rows * 512, rows * width * 10),
        name="local_attention",
    )(qkv, qkv, qkv)


def cross_attention(index, qkv, first, following, last, offset, count):
    rows = qkv.shape[1]
    block = pl.BlockSpec((1, rows + STAT_ROWS, HD), lambda h: (h, 0, 0))
    return pl.pallas_call(
        cross_kernel,
        grid=(count,),
        in_specs=[SMEM]
        + [head_spec(j, rows, offset) for j in range(3)]
        + [
            pl.BlockSpec((2, rows, HD), lambda h: (0, 0, h)),
            pl.BlockSpec((rows, HD), lambda h: (0, h)),
            pl.BlockSpec((rows, HD), lambda h: (0, h)),
        ],
        out_specs=[block] * 3,
        out_shape=[shape((count, rows + STAT_ROWS, HD), BF16)] * 3,
        compiler_params=params(),
        cost_estimate=cost(count * rows * rows * 2560, count * rows * HD * 20),
        name="cross_attention",
    )(index, qkv, qkv, qkv, first, following, last)


def merge_attention(index, local, stats, own, up, far, offset, count, done, width):
    rows = local.shape[1]
    block = pl.BlockSpec((1, rows + STAT_ROWS, HD), lambda h: (h, 0, 0))
    operands = [index, local, stats, own, up, far]
    specs = [
        SMEM,
        pl.BlockSpec((1, rows, HD), lambda h: (h + offset, 0, 0)),
        pl.BlockSpec((1, 8, padded(rows)), lambda h: (h + offset, 0, 0)),
        block,
        block,
        block,
    ]
    aliases = {}
    if done is not None:
        aliases = {len(operands): 0}
        operands.append(done)
        specs.append(pl.BlockSpec(memory_space=pl.ANY))
    return pl.pallas_call(
        merge_kernel,
        grid=(count,),
        in_specs=specs,
        out_specs=pl.BlockSpec((rows, HD), lambda h: (0, h + offset)),
        out_shape=shape((rows, width), BF16),
        input_output_aliases=aliases,
        compiler_params=params(),
        cost_estimate=cost(count * rows * HD * 40, count * rows * HD * 12),
        name="merge_attention",
    )(*operands)


def gathered_attention(attn_qkv):
    rows, width = attn_qkv.shape[1:]
    heads = width // HD
    pairs = lax.all_gather(attn_qkv[1:], "seq", axis=1, tiled=True)
    count = pairs.shape[1]
    query = attn_qkv[0].reshape(rows, heads, HD)
    positions = lax.axis_index("seq") * rows + jnp.arange(rows)
    visible = (jnp.arange(count)[None, :] <= positions[:, None])[None]
    scores = jnp.einsum(
        "qhd,khd->hqk", query, pairs[0].reshape(count, heads, HD), preferred_element_type=F32
    ) / jnp.sqrt(F32(HD))
    scores = jnp.where(visible, scores, F32(-1e30))
    peak = jnp.max(scores, axis=2, keepdims=True)
    weights = jnp.where(visible, jnp.exp(scores - peak), F32(0.0))
    total = jnp.sum(weights, axis=2)
    mixed = jnp.einsum(
        "hqk,khd->qhd",
        weights.astype(BF16),
        pairs[1].reshape(count, heads, HD),
        preferred_element_type=F32,
    )
    return (mixed / total.T[:, :, None]).astype(BF16).reshape(rows, width)


def on_device(se_qkv, se_short, se_filter, mr_qkv, mr_short, mr_filter, mr_decay, attn_qkv):
    rows, width = se_qkv.shape[1:]
    spans = lax.axis_size("seq")
    heads = width // HD
    fwd, inv = (jnp.asarray(m) for m in transforms())
    rising = [(s, s + 1) for s in range(spans - 1)]
    raw = jnp.concatenate(
        [
            se_qkv[1, rows - 8 :],
            se_qkv[2, rows - 8 :],
            se_qkv[0, rows - 2 :],
            mr_qkv[0, rows - 2 :],
            mr_qkv[1, rows - 2 :],
            mr_qkv[2, rows - 2 :],
            jnp.zeros((8, width), BF16),
        ],
        axis=0,
    )
    raw = lax.ppermute(raw, "seq", rising)
    product = mr_tail(mr_qkv, mr_short)
    se_out = se_mixer(se_qkv, raw, se_short, se_filter)
    mr_part, spec, lead = mr_main(mr_qkv, raw, mr_short, mr_filter, mr_decay, fwd, inv)

    if spans == 4:
        index = lax.axis_index("seq").astype(jnp.int32).reshape(1)
        starts = [sum(CHUNKS[:c]) for c in range(len(CHUNKS))]
        local, stats = local_attention(attn_qkv)
        upper = lax.ppermute(product, "seq", [(1, 2), (2, 3)])
        lower = lax.ppermute(product, "seq", [(0, 1)])
        utail = jnp.where(index[0] == 1, lower, upper)
        pieces = []
        for start, count in zip(starts, CHUNKS):
            cols = slice(start * HD, (start + count) * HD)
            first = lax.ppermute(attn_qkv[1:, :, cols], "seq", [(0, 1)])
            asked = attn_qkv[0, :, cols]
            following = lax.ppermute(asked, "seq", [(2, 1), (3, 2)])
            last = lax.ppermute(asked, "seq", [(3, 1)])
            own, up, far = cross_attention(index, attn_qkv, first, following, last, start, count)
            up = lax.ppermute(up, "seq", [(1, 2), (2, 3)])
            far = lax.ppermute(far, "seq", [(1, 3)])
            pieces.append((own, up, far))
        attn_out = None
        for start, count, piece in zip(starts, CHUNKS, pieces):
            attn_out = merge_attention(
                index, local, stats, *piece, start, count, attn_out, width
            )
    else:
        utail = lax.ppermute(product, "seq", rising)
        attn_out = gathered_attention(attn_qkv)
    mr_out = mr_head(utail, lead, spec, mr_qkv, raw, mr_short, fwd, inv, mr_part)
    return (se_out, mr_out, attn_out)


def solution(mesh):
    in_specs = (
        P(None, ("groups", "seq"), "chan"),
        P(None, None, "chan"),
        P(None, "chan"),
        P(None, ("groups", "seq"), "chan"),
        P(None, None, "chan"),
        P(None, "chan"),
        P("chan"),
        P(None, ("groups", "seq"), "chan"),
    )
    out_specs = (
        P(("groups", "seq"), "chan"),
        P(("groups", "seq"), "chan"),
        P(("groups", "seq"), "chan"),
    )
    return jax.shard_map(
        on_device, mesh=mesh, in_specs=in_specs, out_specs=out_specs, check_vma=False
    )
```

```python
import functools

import jax
import jax.numpy as jnp
import ml_dtypes
import numpy as np
from jax import lax
from jax.experimental import pallas as pl
from jax.experimental.pallas import tpu as pltpu
from jax.sharding import PartitionSpec as P

HD = 128
F32 = jnp.float32
BF16 = jnp.bfloat16
SCALE2 = float(np.log2(np.e) / np.sqrt(HD))
PARTS = 4
STAT_ROWS = 16
WINDOW = 256
BLOCK = 128
VMEM_LIMIT = 36 * 1024 * 1024
VMEM_EARLY = 60 * 1024 * 1024


def split_np(value):
    high = value.astype(ml_dtypes.bfloat16)
    low = (value - high.astype(np.float64)).astype(ml_dtypes.bfloat16)
    return high, low


def transforms():
    bins = np.arange(WINDOW // 2)
    omega = 2.0 * np.pi * (bins + 0.5) / WINDOW
    place = np.arange(WINDOW)
    angle = omega[:, None] * place[None, :]
    forward = np.concatenate([np.cos(angle), -np.sin(angle)], axis=0)
    back = (2.0 / WINDOW) * np.concatenate(
        [np.cos(angle[:, BLOCK:]).T, -np.sin(angle[:, BLOCK:]).T], axis=1
    )
    f_high, f_low = split_np(forward)
    b_high, b_low = split_np(back)
    return np.concatenate([f_high, f_low], axis=0), np.concatenate([b_high, b_low], axis=0)


def halves(value):
    high = value.astype(BF16)
    return high, (value - high.astype(F32)).astype(BF16)


def dot(left, right):
    return jnp.dot(left, right, preferred_element_type=F32)


def forward_of(fwd, x_high):
    both = dot(fwd, x_high)
    return both[:WINDOW] + both[WINDOW:]


def spectral(u_spec, f_spec):
    half = WINDOW // 2
    ur, ui = u_spec[:half], u_spec[half:]
    fr, fi = f_spec[:half], f_spec[half:]
    return jnp.concatenate([ur * fr - ui * fi, ur * fi + ui * fr], axis=0)


def back_of(inv, y_spec):
    high, low = halves(y_spec)
    both = dot(inv, high)
    return both[:BLOCK] + both[BLOCK:] + dot(inv[:BLOCK], low)


def featurize(scratch, taps, first, count):
    return (
        taps[0] * scratch[first : first + count]
        + taps[1] * scratch[first - 1 : first - 1 + count]
        + taps[2] * scratch[first - 2 : first - 2 + count]
    )


def tap_rows(short_ref, which):
    return [short_ref[i, which : which + 1, :] for i in range(3)]


def se_kernel(qkv_ref, tail_ref, short_ref, filt_ref, out_ref, q_s, k_s, v_s, u_s):
    rows = qkv_ref.shape[1]
    width = qkv_ref.shape[2]
    tail = tail_ref[...].astype(F32)
    zero = jnp.zeros((8, width), F32)
    k_s[0:8] = zero
    v_s[0:8] = zero
    k_s[8:16] = tail[0:8]
    v_s[8:16] = tail[8:16]
    q_s[0:8] = jnp.concatenate([zero[:6], tail[16:18]], axis=0)
    q_s[8 : 8 + rows] = qkv_ref[0].astype(F32)
    k_s[16 : 16 + rows] = qkv_ref[1].astype(F32)
    v_s[16 : 16 + rows] = qkv_ref[2].astype(F32)
    tq, tk, tv = (tap_rows(short_ref, j) for j in range(3))
    taps = [filt_ref[i : i + 1, :] for i in range(filt_ref.shape[0])]
    u_s[0:8] = featurize(k_s, tk, 8, 8) * featurize(v_s, tv, 8, 8)
    step = 64
    for r in range(0, rows, step):
        u_s[8 + r : 8 + r + step] = featurize(k_s, tk, 16 + r, step) * featurize(
            v_s, tv, 16 + r, step
        )
    for r in range(0, rows, step):
        acc = taps[0] * u_s[8 + r : 8 + r + step]
        for i in range(1, len(taps)):
            acc = acc + taps[i] * u_s[8 + r - i : 8 + r - i + step]
        out_ref[r : r + step] = (featurize(q_s, tq, 8 + r, step) * acc).astype(BF16)


def raw_kernel(se_ref, mr_ref, raw_ref):
    se, mr = se_ref[...].astype(F32), mr_ref[...].astype(F32)
    raw_ref[...] = jnp.concatenate(
        [se[1, 8:], se[2, 8:], se[0, 14:], mr[0, 14:], mr[1, 14:], mr[2, 14:]]
        + [jnp.zeros((8, se.shape[2]), F32)],
        axis=0,
    ).astype(BF16)


def tail_kernel(k_ref, v_ref, short_ref, out_ref, k_s, v_s):
    half = k_ref.shape[1]
    k_s[...] = k_ref[0].astype(F32)
    v_s[...] = v_ref[0].astype(F32)
    tk, tv = tap_rows(short_ref, 1), tap_rows(short_ref, 2)
    first = half - BLOCK
    for r in range(0, BLOCK, 64):
        out_ref[r : r + 64] = (
            featurize(k_s, tk, first + r, 64) * featurize(v_s, tv, first + r, 64)
        ).astype(BF16)


def mr_main_kernel(
    qkv_ref, tail_ref, short_ref, filt_ref, decay_ref, fwd_ref, inv_ref,
    out_ref, spec_ref, lead_ref, q_s, k_s, v_s, u_s,
):
    rows = qkv_ref.shape[1]
    width = qkv_ref.shape[2]
    tail = tail_ref[...].astype(F32)
    zero = jnp.zeros((6, width), F32)
    q_s[0:8] = jnp.concatenate([zero, tail[18:20]], axis=0)
    k_s[0:8] = jnp.concatenate([zero, tail[20:22]], axis=0)
    v_s[0:8] = jnp.concatenate([zero, tail[22:24]], axis=0)
    q_s[8 : 8 + rows] = qkv_ref[0].astype(F32)
    k_s[8 : 8 + rows] = qkv_ref[1].astype(F32)
    v_s[8 : 8 + rows] = qkv_ref[2].astype(F32)
    tq, tk, tv = (tap_rows(short_ref, j) for j in range(3))
    step = 64
    for r in range(0, rows, step):
        u_s[r : r + step] = (
            featurize(k_s, tk, 8 + r, step) * featurize(v_s, tv, 8 + r, step)
        ).astype(BF16)
    lead_ref[...] = u_s[0:BLOCK]
    count = filt_ref.shape[0]
    place = lax.broadcasted_iota(jnp.int32, (count, 1), 0).astype(F32)
    taps = filt_ref[...] * jnp.exp(-decay_ref[...] * place)
    t_high, t_low = halves(taps)
    fwd = fwd_ref[...]
    inv = inv_ref[...]
    spec = forward_of(fwd[:, :count], t_high) + dot(fwd[:WINDOW, :count], t_low)
    spec_ref[...] = spec
    for start in range(BLOCK, rows, BLOCK):
        take = min(BLOCK, rows - start)
        window = BLOCK + take
        u_spec = forward_of(fwd[:, :window], u_s[start - BLOCK : start + take])
        mixed = back_of(inv, spectral(u_spec, spec))
        for r in range(0, take, step):
            out_ref[start + r : start + r + step] = (
                featurize(q_s, tq, 8 + start + r, step) * mixed[r : r + step]
            ).astype(BF16)


def mr_head_kernel(
    idx_ref, low_ref, high_ref, lead_ref, spec_ref, query_ref, tail_ref, short_ref, fwd_ref, inv_ref, part_ref,
    out_ref, q_s,
):
    del part_ref
    width = query_ref.shape[2]
    tail = tail_ref[...].astype(F32)
    q_s[0:8] = jnp.concatenate([jnp.zeros((6, width), F32), tail[18:20]], axis=0)
    q_s[8 : 8 + BLOCK] = query_ref[0].astype(F32)
    tq = tap_rows(short_ref, 0)
    before = jnp.where(idx_ref[0] == 1, low_ref[...].astype(F32), high_ref[...].astype(F32))
    window = jnp.concatenate([before.astype(BF16), lead_ref[...]], axis=0)
    mixed = back_of(inv_ref[...], spectral(forward_of(fwd_ref[...], window), spec_ref[...]))
    for r in range(0, BLOCK, 64):
        out_ref[r : r + 64] = (featurize(q_s, tq, 8 + r, 64) * mixed[r : r + 64]).astype(BF16)


def nt_dot(left, right):
    return lax.dot_general(left, right, (((1,), (1,)), ((), ())), preferred_element_type=F32)


def tt_dot(left, right):
    return lax.dot_general(left, right, (((0,), (0,)), ((), ())), preferred_element_type=F32)


def partials_of(jobs, masked=None):
    scores = [nt_dot(keys, query) for query, keys, _ in jobs]
    if masked is not None:
        key = lax.broadcasted_iota(jnp.int32, scores[0].shape, 0)
        row = lax.broadcasted_iota(jnp.int32, scores[0].shape, 1)
        seen = masked(key, row)
        scores = [jnp.where(seen, s, F32(-1e30)) for s in scores]
    ready = []
    for s in scores:
        peak = jnp.max(s, axis=0, keepdims=True)
        weights = jnp.exp2((s - peak) * SCALE2)
        ready.append((weights.astype(BF16), peak, jnp.sum(weights, axis=0, keepdims=True)))
    results = []
    for (weights, peak, total), (_, _, values) in zip(ready, jobs):
        mixed = tt_dot(values, weights) * (1.0 / total)
        results.append((mixed.T, peak * SCALE2 + jnp.log2(total)))
    return results


def padded(rows):
    return -(-rows // 128) * 128


def pad_rows(value):
    extra = padded(value.shape[0]) - value.shape[0]
    if extra == 0:
        return value
    return jnp.concatenate([value, jnp.zeros((extra, value.shape[1]), value.dtype)], axis=0)


def stat_block(stat):
    high = stat.astype(BF16).astype(F32)
    mid = (stat - high).astype(BF16).astype(F32)
    low = (stat - high - mid).astype(BF16).astype(F32)
    lanes = stat.shape[1] // 128
    parts = [p[:, j * 128 : (j + 1) * 128] for p in (high, mid, low) for j in range(lanes)]
    parts.append(jnp.zeros((STAT_ROWS - len(parts), 128), F32))
    return jnp.concatenate(parts, axis=0).astype(BF16)


def stat_of(block, lanes):
    wide = block.astype(F32)
    total = wide[0:lanes] + wide[lanes : 2 * lanes] + wide[2 * lanes : 3 * lanes]
    return jnp.concatenate([total[j : j + 1] for j in range(lanes)], axis=1)


def put_payload(ref, slot, mixed, stat, rows):
    extra = padded(rows) - rows
    if extra:
        stat = jnp.concatenate([stat[:, :rows], jnp.zeros((1, extra), F32)], axis=1)
    ref[slot, :rows] = mixed[:rows].astype(BF16)
    ref[slot, rows : rows + STAT_ROWS] = stat_block(stat)


def lanes_of(ref, slot, *lead):
    return ref[(*lead, slice(None), slice(slot * HD, (slot + 1) * HD))]


def local_kernel(idx_ref, q_ref, k_ref, v_ref, out_ref, stat_ref):
    rows = q_ref.shape[1]
    slots = range(out_ref.shape[0])

    @pl.when(idx_ref[0] != 1)
    def _():
        jobs = [
            (pad_rows(lanes_of(q_ref, j, 0)), lanes_of(k_ref, j, 0), lanes_of(v_ref, j, 0))
            for j in slots
        ]
        for j, (mixed, stat) in zip(slots, partials_of(jobs, lambda key, row: key <= row)):
            out_ref[j] = mixed[:rows]
            stat_ref[j] = jnp.broadcast_to(stat, stat_ref.shape[1:])


def cross_kernel(has_ahead, has_done, idx_ref, q_ref, k_ref, v_ref, first_ref, *refs):
    if has_ahead:
        ahead_ref, refs = refs[0], refs[1:]
    near_ref, last_ref = refs[:2]
    own_ref, up_ref, far_ref = refs[3 if has_done else 2 :]
    rows = q_ref.shape[1]
    index = idx_ref[0]
    slots = range(up_ref.shape[0])

    @pl.when(index == 1)
    def _():
        jobs = []
        for j in slots:
            query = [lanes_of(q_ref, j, 0), near_ref[j, :rows], last_ref[j, :rows]]
            keys = [lanes_of(first_ref, j, 0), lanes_of(k_ref, j, 0)]
            values = [lanes_of(first_ref, j, 1), lanes_of(v_ref, j, 0)]
            jobs.append(
                (
                    pad_rows(jnp.concatenate(query, axis=0)),
                    jnp.concatenate(keys, axis=0),
                    jnp.concatenate(values, axis=0),
                )
            )
        seen = lambda key, row: (key <= row + rows) | (row >= rows)
        for j, (mixed, stat) in zip(slots, partials_of(jobs, seen)):
            own_ref[:, j * HD : (j + 1) * HD] = mixed[:rows].astype(BF16)
            put_payload(up_ref, j, mixed[rows : 2 * rows], stat[:, rows : 2 * rows], rows)
            put_payload(far_ref, j, mixed[2 * rows : 3 * rows], stat[:, 2 * rows : 3 * rows], rows)

    @pl.when(index == 2)
    def _():
        jobs = [
            (pad_rows(near_ref[j, :rows]), lanes_of(k_ref, j, 0), lanes_of(v_ref, j, 0))
            for j in slots
        ]
        for j, (mixed, stat) in zip(slots, partials_of(jobs)):
            put_payload(up_ref, j, mixed, stat, rows)

    if has_ahead:

        @pl.when(index >= 2)
        def _():
            for j in slots:
                ask = lanes_of(ahead_ref, j, 0)

                far_ref[j, :rows] = ask

                @pl.when(index == 3)
                def _():
                    up_ref[j, :rows] = ask


def merge_kernel(idx_ref, loc_ref, stat_ref, up_ref, far_ref, own_ref, out_ref):
    rows = loc_ref.shape[1]
    lanes = padded(rows) // 128
    index = idx_ref[0]
    slots = range(loc_ref.shape[0])

    def merged(parts):
        for j in slots:
            stats = [stat_ref[j, 0:1]]
            stats += [stat_of(p[j, rows : rows + STAT_ROWS], lanes) for p in parts]
            base = loc_ref[j]
            top = functools.reduce(jnp.maximum, stats)
            weights = [jnp.exp2(s - top) for s in stats]
            scale = 1.0 / functools.reduce(jnp.add, weights)
            result = base
            for weight, part in zip(weights[1:], parts):
                column = jnp.broadcast_to(weight * scale, (128, padded(rows))).T[:rows]
                result = result + column * (part[j, :rows].astype(F32) - base)
            out_ref[:, j * HD : (j + 1) * HD] = result.astype(BF16)

    @pl.when(index == 0)
    def _():
        for j in slots:
            out_ref[:, j * HD : (j + 1) * HD] = loc_ref[j].astype(BF16)

    @pl.when(index == 1)
    def _():
        out_ref[...] = own_ref[...]

    @pl.when(index == 2)
    def _():
        merged([up_ref])

    @pl.when(index == 3)
    def _():
        merged([up_ref, far_ref])


def pack_kernel(lows, asks, part, idx_ref, qkv_ref, *refs):
    low_refs, ask_refs = refs[: len(lows)], refs[len(lows) : len(lows) + len(asks)]
    low_s, ask_s, sems = refs[len(lows) + len(asks) :]
    rows = qkv_ref.shape[1]
    heads = part // HD
    index = idx_ref[0]

    def cols(c):
        return pl.ds(c * part, part)

    def move(steps):
        loads, stores = [], []
        for source, place, targets in steps:
            load = pltpu.make_async_copy(source, place, sems.at[0, len(loads)])
            load.start()
            loads.append(load)
        for load, (_, _, targets) in zip(loads, steps):
            load.wait()
            for source, target in targets:
                store = pltpu.make_async_copy(source, target, sems.at[1, len(stores)])
                store.start()
                stores.append(store)
        for store in stores:
            store.wait()

    def ask_steps():
        return [
            (
                qkv_ref.at[0, :, cols(c)],
                ask_s.at[i],
                [
                    (ask_s.at[i, :, pl.ds(h * HD, HD)], ask_refs[i].at[h, pl.ds(0, rows), :])
                    for h in range(heads)
                ],
            )
            for i, c in enumerate(asks)
        ]

    @pl.when(index == 0)
    def _():
        move(
            [
                (qkv_ref.at[1:3, :, cols(c)], low_s.at[i], [(low_s.at[i], low_refs[i])])
                for i, c in enumerate(lows)
            ]
        )

    if asks:

        @pl.when(index >= 2)
        def _():
            move(ask_steps())


def params(limit=VMEM_LIMIT):
    return pltpu.CompilerParams(vmem_limit_bytes=limit)


def cost(flops, size):
    return pl.CostEstimate(flops=1, bytes_accessed=1, transcendentals=0)


SMEM = pl.BlockSpec(memory_space=pltpu.SMEM)


def shape(dims, kind):
    return jax.ShapeDtypeStruct(dims, kind)


def full(array):
    return pl.BlockSpec(array.shape, lambda j: (0,) * array.ndim)


def se_mixer(qkv, tail, short, filt):
    rows, width = qkv.shape[1:]
    cols = 256
    return pl.pallas_call(
        se_kernel,
        grid=(width // cols,),
        in_specs=[
            pl.BlockSpec((3, rows, cols), lambda j: (0, 0, j)),
            pl.BlockSpec((tail.shape[0], cols), lambda j: (0, j)),
            pl.BlockSpec((3, 3, cols), lambda j: (0, 0, j)),
            pl.BlockSpec((filt.shape[0], cols), lambda j: (0, j)),
        ],
        out_specs=pl.BlockSpec((rows, cols), lambda j: (0, j)),
        out_shape=shape((rows, width), BF16),
        scratch_shapes=[
            pltpu.VMEM((8 + rows, cols), F32),
            pltpu.VMEM((16 + rows, cols), F32),
            pltpu.VMEM((16 + rows, cols), F32),
            pltpu.VMEM((8 + rows, cols), F32),
        ],
        compiler_params=params(),
        cost_estimate=cost(rows * width * 40, rows * width * 8),
        name="se_mixer",
    )(qkv, tail, short, filt)


def raw_of(se_qkv, mr_qkv):
    rows, width = mr_qkv.shape[1:]
    last = rows // 16 - 1
    tail = pl.BlockSpec((3, 16, width), lambda j: (0, last, 0))
    return pl.pallas_call(
        raw_kernel,
        grid=(1,),
        in_specs=[tail, tail],
        out_specs=pl.BlockSpec((32, width), lambda j: (0, 0)),
        out_shape=shape((32, width), BF16),
        compiler_params=params(VMEM_EARLY),
        cost_estimate=cost(0, 0),
        name="raw_tail",
    )(se_qkv, mr_qkv)


def product_of(mr_qkv, short):
    rows, width = mr_qkv.shape[1:]
    cols = min(1024, width)
    half = rows // 2
    return pl.pallas_call(
        tail_kernel,
        grid=(width // cols,),
        in_specs=[
            pl.BlockSpec((1, half, cols), lambda j: (1, 1, j)),
            pl.BlockSpec((1, half, cols), lambda j: (2, 1, j)),
            pl.BlockSpec((3, 3, cols), lambda j: (0, 0, j)),
        ],
        out_specs=pl.BlockSpec((BLOCK, cols), lambda j: (0, j)),
        out_shape=shape((BLOCK, width), BF16),
        scratch_shapes=[pltpu.VMEM((half, cols), F32), pltpu.VMEM((half, cols), F32)],
        compiler_params=params(VMEM_EARLY),
        cost_estimate=cost(BLOCK * width * 12, rows * width * 3),
        name="product_tail",
    )(mr_qkv, mr_qkv, short)


def pack(index, qkv, lows, asks):
    rows, width = qkv.shape[1:]
    count = width // HD // PARTS
    part = count * HD
    anywhere = pl.BlockSpec(memory_space=pl.ANY)
    total = len(lows) + len(asks)
    out = pl.pallas_call(
        functools.partial(pack_kernel, lows, asks, part),
        in_specs=[SMEM, anywhere],
        out_specs=[anywhere] * total,
        out_shape=[shape((2, rows, part), BF16)] * len(lows)
        + [shape((count, rows + STAT_ROWS, HD), BF16)] * len(asks),
        scratch_shapes=[
            pltpu.VMEM((max(len(lows), 1), 2, rows, part), BF16),
            pltpu.VMEM((max(len(asks), 1), rows, part), BF16),
            pltpu.SemaphoreType.DMA((2, len(lows) + len(asks) * count)),
        ],
        compiler_params=params(VMEM_EARLY),
        cost_estimate=cost(0, 0),
        name="pack",
    )(index, qkv)
    return out[: len(lows)], out[len(lows) :]


def mr_main(qkv, tail, short, filt, decay, fwd, inv):
    rows, width = qkv.shape[1:]
    cols = 512
    col = lambda j: (0, j)
    return pl.pallas_call(
        mr_main_kernel,
        grid=(width // cols,),
        in_specs=[
            pl.BlockSpec((3, rows, cols), lambda j: (0, 0, j)),
            pl.BlockSpec((tail.shape[0], cols), col),
            pl.BlockSpec((3, 3, cols), lambda j: (0, 0, j)),
            pl.BlockSpec((filt.shape[0], cols), col),
            pl.BlockSpec((1, cols), col),
            full(fwd),
            full(inv),
        ],
        out_specs=[
            pl.BlockSpec((rows, cols), col),
            pl.BlockSpec((WINDOW, cols), col),
            pl.BlockSpec((BLOCK, cols), col),
        ],
        out_shape=[
            shape((rows, width), BF16),
            shape((WINDOW, width), F32),
            shape((BLOCK, width), BF16),
        ],
        scratch_shapes=[pltpu.VMEM((8 + rows, cols), F32)] * 3 + [pltpu.VMEM((rows, cols), BF16)],
        compiler_params=params(),
        cost_estimate=cost(WINDOW * WINDOW * width * 16, rows * width * 14),
        name="mr_main",
    )(qkv, tail, short, filt, decay[None, :], fwd, inv)


def mr_head(index, low, high, lead, spec, qkv, tail, short, fwd, inv, part):
    rows, width = qkv.shape[1:]
    cols = 512
    col = lambda j: (0, j)
    return pl.pallas_call(
        mr_head_kernel,
        grid=(width // cols,),
        in_specs=[
            SMEM,
            pl.BlockSpec((BLOCK, cols), col),
            pl.BlockSpec((BLOCK, cols), col),
            pl.BlockSpec((BLOCK, cols), col),
            pl.BlockSpec((WINDOW, cols), col),
            pl.BlockSpec((1, BLOCK, cols), lambda j: (0, 0, j)),
            pl.BlockSpec((tail.shape[0], cols), col),
            pl.BlockSpec((3, 3, cols), lambda j: (0, 0, j)),
            full(fwd),
            full(inv),
            pl.BlockSpec(memory_space=pl.ANY),
        ],
        out_specs=pl.BlockSpec((BLOCK, cols), col),
        out_shape=shape((rows, width), BF16),
        scratch_shapes=[pltpu.VMEM((8 + BLOCK, cols), F32)],
        input_output_aliases={10: 0},
        compiler_params=params(),
        cost_estimate=cost(WINDOW * WINDOW * width * 6, rows * width * 4),
        name="mr_head",
    )(index, low, high, lead, spec, qkv, tail, short, fwd, inv, part)


def per_step(count):
    return 2 if count % 2 == 0 else 1


def head_spec(which, rows, per, offset):
    return pl.BlockSpec((1, rows, per * HD), lambda h: (which, 0, h + offset // per))


def unless_first(place):
    return lambda h, idx: jnp.where(idx[0] == 1, 0, h + place)


def local_attention(index, qkv):
    rows, width = qkv.shape[1:]
    heads = width // HD
    per = 4 if heads % 4 == 0 else 1
    at = unless_first(0)

    def part(which):
        return pl.BlockSpec((1, rows, per * HD), lambda h, idx: (which, 0, at(h, idx)))

    return pl.pallas_call(
        local_kernel,
        grid_spec=pltpu.PrefetchScalarGridSpec(
            num_scalar_prefetch=1,
            grid=(heads // per,),
            in_specs=[part(j) for j in range(3)],
            out_specs=[
                pl.BlockSpec((per, rows, HD), lambda h, idx: (at(h, idx), 0, 0)),
                pl.BlockSpec((per, 8, padded(rows)), lambda h, idx: (at(h, idx), 0, 0)),
            ],
        ),
        out_shape=[shape((heads, rows, HD), F32), shape((heads, 8, padded(rows)), F32)],
        compiler_params=params(),
        cost_estimate=cost(heads * rows * rows * 512, rows * width * 10),
        name="local_attention",
    )(index, qkv, qkv, qkv)


def cross_attention(index, qkv, first, near, last, done, c):
    rows, width = qkv.shape[1:]
    count = width // HD // PARTS
    per = per_step(count)
    steps = count // per
    block = pl.BlockSpec((per, rows + STAT_ROWS, HD), lambda h: (h, 0, 0))
    has_ahead = c + 2 < PARTS

    def part(which, chunk):
        return pl.BlockSpec((1, rows, per * HD), lambda h: (which, 0, h + chunk * steps))

    specs = [SMEM] + [part(j, c) for j in range(3)]
    specs.append(pl.BlockSpec((2, rows, per * HD), lambda h: (0, 0, h)))
    operands = [index, qkv, qkv, qkv, first]
    if has_ahead:
        specs.append(part(0, c + 2))
        operands.append(qkv)
    operands += [near, last]
    specs += [block, block]
    aliases = {}
    if done is not None:
        aliases = {len(operands): 0}
        operands.append(done)
        specs.append(pl.BlockSpec(memory_space=pl.ANY))
    return pl.pallas_call(
        functools.partial(cross_kernel, has_ahead, done is not None),
        grid=(steps,),
        in_specs=specs,
        out_specs=[pl.BlockSpec((rows, per * HD), lambda h: (0, h + c * steps)), block, block],
        out_shape=[shape((rows, width), BF16)]
        + [shape((count, rows + STAT_ROWS, HD), BF16)] * 2,
        input_output_aliases=aliases,
        compiler_params=params(),
        cost_estimate=cost(count * rows * rows * 3072, count * rows * HD * 20),
        name="cross_attention",
    )(*operands)


def merge_attention(index, local, stats, up, far, done, c):
    rows, width = done.shape
    count = width // HD // PARTS
    per = per_step(count)
    steps = count // per
    here, there = unless_first(0), unless_first(c * steps)
    block = pl.BlockSpec((per, rows + STAT_ROWS, HD), lambda h, idx: (here(h, idx), 0, 0))
    flat = pl.BlockSpec((rows, per * HD), lambda h, idx: (0, there(h, idx)))
    return pl.pallas_call(
        merge_kernel,
        grid_spec=pltpu.PrefetchScalarGridSpec(
            num_scalar_prefetch=1,
            grid=(steps,),
            in_specs=[
                pl.BlockSpec((per, rows, HD), lambda h, idx: (there(h, idx), 0, 0)),
                pl.BlockSpec((per, 8, padded(rows)), lambda h, idx: (there(h, idx), 0, 0)),
                block,
                block,
                flat,
            ],
            out_specs=flat,
        ),
        out_shape=shape((rows, width), BF16),
        input_output_aliases={5: 0},
        compiler_params=params(),
        cost_estimate=cost(count * rows * HD * 40, count * rows * HD * 12),
        name="merge_attention",
    )(index, local, stats, up, far, done)


def gathered_attention(attn_qkv):
    rows, width = attn_qkv.shape[1:]
    heads = width // HD
    pairs = lax.all_gather(attn_qkv[1:], "seq", axis=1, tiled=True)
    count = pairs.shape[1]
    query = attn_qkv[0].reshape(rows, heads, HD)
    positions = lax.axis_index("seq") * rows + jnp.arange(rows)
    visible = (jnp.arange(count)[None, :] <= positions[:, None])[None]
    scores = jnp.einsum(
        "qhd,khd->hqk", query, pairs[0].reshape(count, heads, HD), preferred_element_type=F32
    ) / jnp.sqrt(F32(HD))
    scores = jnp.where(visible, scores, F32(-1e30))
    peak = jnp.max(scores, axis=2, keepdims=True)
    weights = jnp.where(visible, jnp.exp(scores - peak), F32(0.0))
    total = jnp.sum(weights, axis=2)
    mixed = jnp.einsum(
        "hqk,khd->qhd",
        weights.astype(BF16),
        pairs[1].reshape(count, heads, HD),
        preferred_element_type=F32,
    )
    return (mixed / total.T[:, :, None]).astype(BF16).reshape(rows, width)


def after(value, *needed):
    return lax.optimization_barrier((value,) + needed)[0]


def on_device(se_qkv, se_short, se_filter, mr_qkv, mr_short, mr_filter, mr_decay, attn_qkv):
    rows, width = se_qkv.shape[1:]
    spans = lax.axis_size("seq")
    fwd, inv = (jnp.asarray(m) for m in transforms())
    rising = [(s, s + 1) for s in range(spans - 1)]
    if spans == 4 and width % (PARTS * HD) == 0:
        return four_spans(
            se_qkv, se_short, se_filter, mr_qkv, mr_short, mr_filter, mr_decay, attn_qkv, fwd, inv
        )
    raw = lax.ppermute(raw_of(se_qkv, mr_qkv), "seq", rising)
    product = product_of(mr_qkv, mr_short)
    se_out = se_mixer(se_qkv, raw, se_short, se_filter)
    mr_part, spec, lead = mr_main(mr_qkv, raw, mr_short, mr_filter, mr_decay, fwd, inv)
    utail = lax.ppermute(product, "seq", rising)
    attn_out = gathered_attention(attn_qkv)
    index = lax.axis_index("seq").astype(jnp.int32).reshape(1)
    mr_out = mr_head(
        index, utail, utail, lead, spec, mr_qkv, raw, mr_short, fwd, inv, mr_part
    )
    return (se_out, mr_out, attn_out)


def four_spans(
    se_qkv, se_short, se_filter, mr_qkv, mr_short, mr_filter, mr_decay, attn_qkv, fwd, inv
):
    width = attn_qkv.shape[2]
    count = width // HD // PARTS
    send = lambda value, *pairs: lax.ppermute(value, "seq", list(pairs))
    index = lax.axis_index("seq").astype(jnp.int32).reshape(1)
    raw_own = raw_of(se_qkv, mr_qkv)
    raw = send(raw_own, (0, 1), (1, 2), (2, 3))
    a_in, ask_in = pack(index, after(attn_qkv, raw_own), [0], [0])
    a, b, d, up, far = ({} for _ in range(5))
    from_above = [(2, 1), (3, 2)]
    merging = [(1, 2), (2, 3)]
    b[0] = send(ask_in[0], (3, 1))
    d[0] = send(ask_in[0], *from_above)
    a[0] = send(a_in[0], (0, 1))
    product = product_of(after(mr_qkv, a_in[0], raw), mr_short)
    upper = send(product, (1, 2), (2, 3))
    later = pack(index, after(attn_qkv, product), [1, 2, 3], [1])
    a_in, ask_in = a_in + later[0], ask_in + later[1]
    se_out = se_mixer(after(se_qkv, a_in[1]), raw, se_short, se_filter)
    local, stats = local_attention(index, after(attn_qkv, se_out, b[0], d[0]))

    def cross(c, done, *needed):
        return cross_attention(index, attn_qkv, after(a[c], *needed), d[c], b[c], done, c)

    a[1] = send(after(a_in[1], raw), (0, 1))
    b[1] = send(after(ask_in[1], b[0], d[0], se_out), (3, 1))
    d[1] = send(after(ask_in[1], b[0], d[0], se_out), *from_above)
    attn_out, up[0], far[0] = cross(0, None, upper, stats)
    b[2] = send(up[0], (3, 1), *merging)
    d[2] = send(far[0], (1, 3), *from_above)
    a[2] = send(after(a_in[2], a[1]), (0, 1))
    a[3] = send(after(a_in[3], a[1], b[1], d[1], up[0]), (0, 1))
    attn_out, up[1], far[1] = cross(1, attn_out)
    b[3] = send(up[1], (3, 1), *merging)
    d[3] = send(after(far[1], b[2]), (1, 3), *from_above)
    lower = send(after(product, a[2], up[1]), (0, 1))
    attn_out, up[2], far[2] = cross(2, attn_out)
    b[4] = send(up[2], *merging)
    d[4] = send(after(far[2], b[3]), (1, 3))
    attn_out, up[3], far[3] = cross(3, attn_out)
    b[5] = send(up[3], *merging)
    d[5] = send(far[3], (1, 3))
    mr_part, spec, lead = mr_main(
        after(mr_qkv, attn_out), raw, mr_short, mr_filter, mr_decay, fwd, inv
    )
    for c in range(PARTS):
        if c == PARTS - 1:
            mr_out = mr_head(
                index, lower, upper, lead, spec, mr_qkv, raw, mr_short, fwd, inv, mr_part
            )
            local = after(local, mr_out)
        attn_out = merge_attention(
            index, after(local, lead), stats, b[c + 2], d[c + 2], attn_out, c
        )
    return (se_out, mr_out, attn_out)


def solution(mesh):
    in_specs = (
        P(None, ("groups", "seq"), "chan"),
        P(None, None, "chan"),
        P(None, "chan"),
        P(None, ("groups", "seq"), "chan"),
        P(None, None, "chan"),
        P(None, "chan"),
        P("chan"),
        P(None, ("groups", "seq"), "chan"),
    )
    out_specs = (
        P(("groups", "seq"), "chan"),
        P(("groups", "seq"), "chan"),
        P(("groups", "seq"), "chan"),
    )
    return jax.shard_map(
        on_device, mesh=mesh, in_specs=in_specs, out_specs=out_specs, check_vma=False
    )
```

```python
import functools

import jax
import jax.numpy as jnp
import ml_dtypes
import numpy as np
from jax import lax
from jax.experimental import pallas as pl
from jax.experimental.pallas import tpu as pltpu
from jax.sharding import PartitionSpec as P

HD = 128
F32 = jnp.float32
BF16 = jnp.bfloat16
SCALE2 = float(np.log2(np.e) / np.sqrt(HD))
PARTS = 4
STAT_ROWS = 16
WINDOW = 256
BLOCK = 128
VMEM_LIMIT = 36 * 1024 * 1024
VMEM_EARLY = 60 * 1024 * 1024


def split_np(value):
    high = value.astype(ml_dtypes.bfloat16)
    low = (value - high.astype(np.float64)).astype(ml_dtypes.bfloat16)
    return high, low


def transforms():
    bins = np.arange(WINDOW // 2)
    omega = 2.0 * np.pi * (bins + 0.5) / WINDOW
    place = np.arange(WINDOW)
    angle = omega[:, None] * place[None, :]
    forward = np.concatenate([np.cos(angle), -np.sin(angle)], axis=0)
    back = (2.0 / WINDOW) * np.concatenate(
        [np.cos(angle[:, BLOCK:]).T, -np.sin(angle[:, BLOCK:]).T], axis=1
    )
    f_high, f_low = split_np(forward)
    b_high, b_low = split_np(back)
    return np.concatenate([f_high, f_low], axis=0), np.concatenate([b_high, b_low], axis=0)


def halves(value):
    high = value.astype(BF16)
    return high, (value - high.astype(F32)).astype(BF16)


def dot(left, right):
    return jnp.dot(left, right, preferred_element_type=F32)


def forward_of(fwd, x_high):
    both = dot(fwd, x_high)
    return both[:WINDOW] + both[WINDOW:]


def spectral(u_spec, f_spec):
    half = WINDOW // 2
    ur, ui = u_spec[:half], u_spec[half:]
    fr, fi = f_spec[:half], f_spec[half:]
    return jnp.concatenate([ur * fr - ui * fi, ur * fi + ui * fr], axis=0)


def back_of(inv, y_spec):
    high, low = halves(y_spec)
    both = dot(inv, high)
    return both[:BLOCK] + both[BLOCK:] + dot(inv[:BLOCK], low)


def featurize(scratch, taps, first, count):
    return (
        taps[0] * scratch[first : first + count]
        + taps[1] * scratch[first - 1 : first - 1 + count]
        + taps[2] * scratch[first - 2 : first - 2 + count]
    )


def tap_rows(short_ref, which):
    return [short_ref[i, which : which + 1, :] for i in range(3)]


def se_kernel(qkv_ref, tail_ref, short_ref, filt_ref, out_ref, q_s, k_s, v_s, u_s):
    rows = qkv_ref.shape[1]
    width = qkv_ref.shape[2]
    tail = tail_ref[...].astype(F32)
    zero = jnp.zeros((8, width), F32)
    k_s[0:8] = zero
    v_s[0:8] = zero
    k_s[8:16] = tail[0:8]
    v_s[8:16] = tail[8:16]
    q_s[0:8] = jnp.concatenate([zero[:6], tail[16:18]], axis=0)
    q_s[8 : 8 + rows] = qkv_ref[0].astype(F32)
    k_s[16 : 16 + rows] = qkv_ref[1].astype(F32)
    v_s[16 : 16 + rows] = qkv_ref[2].astype(F32)
    tq, tk, tv = (tap_rows(short_ref, j) for j in range(3))
    taps = [filt_ref[i : i + 1, :] for i in range(filt_ref.shape[0])]
    u_s[0:8] = featurize(k_s, tk, 8, 8) * featurize(v_s, tv, 8, 8)
    step = 64
    for r in range(0, rows, step):
        u_s[8 + r : 8 + r + step] = featurize(k_s, tk, 16 + r, step) * featurize(
            v_s, tv, 16 + r, step
        )
    for r in range(0, rows, step):
        acc = taps[0] * u_s[8 + r : 8 + r + step]
        for i in range(1, len(taps)):
            acc = acc + taps[i] * u_s[8 + r - i : 8 + r - i + step]
        out_ref[r : r + step] = (featurize(q_s, tq, 8 + r, step) * acc).astype(BF16)


def raw_kernel(se_ref, mr_ref, raw_ref):
    se, mr = se_ref[...].astype(F32), mr_ref[...].astype(F32)
    raw_ref[...] = jnp.concatenate(
        [se[1, 8:], se[2, 8:], se[0, 14:], mr[0, 14:], mr[1, 14:], mr[2, 14:]]
        + [jnp.zeros((8, se.shape[2]), F32)],
        axis=0,
    ).astype(BF16)


def tail_kernel(k_ref, v_ref, short_ref, out_ref, k_s, v_s):
    half = k_ref.shape[1]
    k_s[...] = k_ref[0].astype(F32)
    v_s[...] = v_ref[0].astype(F32)
    tk, tv = tap_rows(short_ref, 1), tap_rows(short_ref, 2)
    first = half - BLOCK
    for r in range(0, BLOCK, 64):
        out_ref[r : r + 64] = (
            featurize(k_s, tk, first + r, 64) * featurize(v_s, tv, first + r, 64)
        ).astype(BF16)


def mr_main_kernel(
    qkv_ref, tail_ref, short_ref, filt_ref, decay_ref, fwd_ref, inv_ref,
    out_ref, spec_ref, lead_ref, q_s, k_s, v_s, u_s,
):
    rows = qkv_ref.shape[1]
    width = qkv_ref.shape[2]
    tail = tail_ref[...].astype(F32)
    zero = jnp.zeros((6, width), F32)
    q_s[0:8] = jnp.concatenate([zero, tail[18:20]], axis=0)
    k_s[0:8] = jnp.concatenate([zero, tail[20:22]], axis=0)
    v_s[0:8] = jnp.concatenate([zero, tail[22:24]], axis=0)
    q_s[8 : 8 + rows] = qkv_ref[0].astype(F32)
    k_s[8 : 8 + rows] = qkv_ref[1].astype(F32)
    v_s[8 : 8 + rows] = qkv_ref[2].astype(F32)
    tq, tk, tv = (tap_rows(short_ref, j) for j in range(3))
    step = 64
    for r in range(0, rows, step):
        u_s[r : r + step] = (
            featurize(k_s, tk, 8 + r, step) * featurize(v_s, tv, 8 + r, step)
        ).astype(BF16)
    lead_ref[...] = u_s[0:BLOCK]
    count = filt_ref.shape[0]
    place = lax.broadcasted_iota(jnp.int32, (count, 1), 0).astype(F32)
    taps = filt_ref[...] * jnp.exp(-decay_ref[...] * place)
    t_high, t_low = halves(taps)
    fwd = fwd_ref[...]
    inv = inv_ref[...]
    spec = forward_of(fwd[:, :count], t_high) + dot(fwd[:WINDOW, :count], t_low)
    spec_ref[...] = spec
    for start in range(BLOCK, rows, BLOCK):
        take = min(BLOCK, rows - start)
        window = BLOCK + take
        u_spec = forward_of(fwd[:, :window], u_s[start - BLOCK : start + take])
        mixed = back_of(inv, spectral(u_spec, spec))
        for r in range(0, take, step):
            out_ref[start + r : start + r + step] = (
                featurize(q_s, tq, 8 + start + r, step) * mixed[r : r + step]
            ).astype(BF16)


def mr_head_kernel(
    idx_ref, low_ref, high_ref, lead_ref, spec_ref, query_ref, tail_ref, short_ref, fwd_ref, inv_ref, part_ref,
    out_ref, q_s,
):
    del part_ref
    width = query_ref.shape[2]
    tail = tail_ref[...].astype(F32)
    q_s[0:8] = jnp.concatenate([jnp.zeros((6, width), F32), tail[18:20]], axis=0)
    q_s[8 : 8 + BLOCK] = query_ref[0].astype(F32)
    tq = tap_rows(short_ref, 0)
    before = jnp.where(idx_ref[0] == 1, low_ref[...].astype(F32), high_ref[...].astype(F32))
    window = jnp.concatenate([before.astype(BF16), lead_ref[...]], axis=0)
    mixed = back_of(inv_ref[...], spectral(forward_of(fwd_ref[...], window), spec_ref[...]))
    for r in range(0, BLOCK, 64):
        out_ref[r : r + 64] = (featurize(q_s, tq, 8 + r, 64) * mixed[r : r + 64]).astype(BF16)


def nt_dot(left, right):
    return lax.dot_general(left, right, (((1,), (1,)), ((), ())), preferred_element_type=F32)


def tt_dot(left, right):
    return lax.dot_general(left, right, (((0,), (0,)), ((), ())), preferred_element_type=F32)


def partials_of(jobs, masked=None):
    scores = [nt_dot(keys, query) for query, keys, _ in jobs]
    if masked is not None:
        key = lax.broadcasted_iota(jnp.int32, scores[0].shape, 0)
        row = lax.broadcasted_iota(jnp.int32, scores[0].shape, 1)
        seen = masked(key, row)
        scores = [jnp.where(seen, s, F32(-1e30)) for s in scores]
    ready = []
    for s in scores:
        peak = jnp.max(s, axis=0, keepdims=True)
        weights = jnp.exp2((s - peak) * SCALE2)
        ready.append((weights.astype(BF16), peak, jnp.sum(weights, axis=0, keepdims=True)))
    results = []
    for (weights, peak, total), (_, _, values) in zip(ready, jobs):
        mixed = tt_dot(values, weights) * (1.0 / total)
        results.append((mixed.T, peak * SCALE2 + jnp.log2(total)))
    return results


def padded(rows):
    return -(-rows // 128) * 128


def pad_rows(value):
    extra = padded(value.shape[0]) - value.shape[0]
    if extra == 0:
        return value
    return jnp.concatenate([value, jnp.zeros((extra, value.shape[1]), value.dtype)], axis=0)


def put_payload(ref, mixes, stats, rows):
    for j, mixed in enumerate(mixes):
        ref[0, j * rows : (j + 1) * rows] = mixed[:rows].astype(BF16)
    total = len(mixes) * rows
    extra = padded(total) - total
    parts = [s[:, :rows] for s in stats] + ([jnp.zeros((1, extra), F32)] if extra else [])
    stat = jnp.concatenate(parts, axis=1)
    high = stat.astype(BF16).astype(F32)
    mid = (stat - high).astype(BF16).astype(F32)
    low = (stat - high - mid).astype(BF16).astype(F32)
    lanes = padded(total) // 128
    pieces = [p[:, j * 128 : (j + 1) * 128] for p in (high, mid, low) for j in range(lanes)]
    spare = STAT_ROWS - len(pieces)
    pieces += [jnp.zeros((spare, 128), F32)] if spare else []
    ref[0, total : total + STAT_ROWS] = jnp.concatenate(pieces, axis=0).astype(BF16)


def stats_from(ref, count, rows):
    total = count * rows
    lanes = padded(total) // 128
    wide = ref[0, total : total + STAT_ROWS].astype(F32)
    added = wide[0:lanes] + wide[lanes : 2 * lanes] + wide[2 * lanes : 3 * lanes]
    row = [added[j : j + 1] for j in range(lanes)] + [jnp.zeros((1, padded(rows)), F32)]
    row = jnp.concatenate(row, axis=1)
    return [row[:, j * rows : j * rows + padded(rows)] for j in range(count)]


def lanes_of(ref, slot, *lead):
    return ref[(*lead, slice(None), slice(slot * HD, (slot + 1) * HD))]


def local_kernel(idx_ref, q_ref, k_ref, v_ref, out_ref, stat_ref):
    rows = q_ref.shape[1]
    slots = range(out_ref.shape[0])

    @pl.when(idx_ref[0] != 1)
    def _():
        jobs = [
            (pad_rows(lanes_of(q_ref, j, 0)), lanes_of(k_ref, j, 0), lanes_of(v_ref, j, 0))
            for j in slots
        ]
        for j, (mixed, stat) in zip(slots, partials_of(jobs, lambda key, row: key <= row)):
            out_ref[j] = mixed[:rows]
            stat_ref[j] = jnp.broadcast_to(stat, stat_ref.shape[1:])


def cross_kernel(has_ahead, has_done, idx_ref, q_ref, k_ref, v_ref, first_ref, *refs):
    if has_ahead:
        ahead_ref, refs = refs[0], refs[1:]
    near_ref, last_ref = refs[:2]
    own_ref, up_ref, far_ref = refs[3 if has_done else 2 :]
    rows = q_ref.shape[1]
    index = idx_ref[0]
    slots = range(q_ref.shape[2] // HD)

    def slot(ref, j):
        return ref[0, j * rows : (j + 1) * rows]

    @pl.when(index == 1)
    def _():
        jobs = []
        for j in slots:
            query = [lanes_of(q_ref, j, 0), slot(near_ref, j), slot(last_ref, j)]
            keys = [lanes_of(first_ref, j, 0), lanes_of(k_ref, j, 0)]
            values = [lanes_of(first_ref, j, 1), lanes_of(v_ref, j, 0)]
            jobs.append(
                (
                    pad_rows(jnp.concatenate(query, axis=0)),
                    jnp.concatenate(keys, axis=0),
                    jnp.concatenate(values, axis=0),
                )
            )
        seen = lambda key, row: (key <= row + rows) | (row >= rows)
        results = partials_of(jobs, seen)
        for j, (mixed, _) in zip(slots, results):
            own_ref[:, j * HD : (j + 1) * HD] = mixed[:rows].astype(BF16)
        for ref, start in ((up_ref, rows), (far_ref, 2 * rows)):
            put_payload(
                ref,
                [mixed[start : start + rows] for mixed, _ in results],
                [stat[:, start : start + rows] for _, stat in results],
                rows,
            )

    @pl.when(index == 2)
    def _():
        jobs = [
            (pad_rows(slot(near_ref, j)), lanes_of(k_ref, j, 0), lanes_of(v_ref, j, 0))
            for j in slots
        ]
        results = partials_of(jobs)
        put_payload(up_ref, [m for m, _ in results], [t for _, t in results], rows)

    if has_ahead:

        @pl.when(index >= 2)
        def _():
            for j in slots:
                ask = lanes_of(ahead_ref, j, 0)

                far_ref[0, j * rows : (j + 1) * rows] = ask

                @pl.when(index == 3)
                def _():
                    up_ref[0, j * rows : (j + 1) * rows] = ask


def merge_kernel(steps, parts, idx_ref, loc_ref, stat_ref, *refs):
    ups, fars = refs[:parts], refs[parts : 2 * parts]
    own_ref, out_ref = refs[2 * parts :]
    rows = loc_ref.shape[1]
    index = idx_ref[0]
    slots = range(loc_ref.shape[0])
    chunk = pl.program_id(0) // steps

    def merged(sent):
        known = [stats_from(p, len(slots), rows) for p in sent]
        for j in slots:
            stats = [stat_ref[j, 0:1]] + [k[j] for k in known]
            base = loc_ref[j]
            top = functools.reduce(jnp.maximum, stats)
            weights = [jnp.exp2(s - top) for s in stats]
            scale = 1.0 / functools.reduce(jnp.add, weights)
            result = base
            for weight, part in zip(weights[1:], sent):
                column = jnp.broadcast_to(weight * scale, (128, padded(rows))).T[:rows]
                result = result + column * (part[0, j * rows : (j + 1) * rows].astype(F32) - base)
            out_ref[:, j * HD : (j + 1) * HD] = result.astype(BF16)

    @pl.when(index == 0)
    def _():
        for j in slots:
            out_ref[:, j * HD : (j + 1) * HD] = loc_ref[j].astype(BF16)

    @pl.when(index == 1)
    def _():
        out_ref[...] = own_ref[...]

    for c in range(parts):

        @pl.when((index == 2) & (chunk == c))
        def _():
            merged([ups[c]])

        @pl.when((index == 3) & (chunk == c))
        def _():
            merged([ups[c], fars[c]])


def pack_kernel(lows, asks, part, idx_ref, qkv_ref, *refs):
    low_refs, ask_refs = refs[: len(lows)], refs[len(lows) : len(lows) + len(asks)]
    low_s, ask_s, sems = refs[len(lows) + len(asks) :]
    rows = qkv_ref.shape[1]
    heads = part // HD
    per = per_step(heads)
    index = idx_ref[0]

    def cols(c):
        return pl.ds(c * part, part)

    def move(steps):
        loads, stores = [], []
        for source, place, targets in steps:
            load = pltpu.make_async_copy(source, place, sems.at[0, len(loads)])
            load.start()
            loads.append(load)
        for load, (_, _, targets) in zip(loads, steps):
            load.wait()
            for source, target in targets:
                store = pltpu.make_async_copy(source, target, sems.at[1, len(stores)])
                store.start()
                stores.append(store)
        for store in stores:
            store.wait()

    def ask_steps():
        return [
            (
                qkv_ref.at[0, :, cols(c)],
                ask_s.at[i],
                [
                    (
                        ask_s.at[i, :, pl.ds(h * HD, HD)],
                        ask_refs[i].at[h // per, pl.ds(h % per * rows, rows), :],
                    )
                    for h in range(heads)
                ],
            )
            for i, c in enumerate(asks)
        ]

    @pl.when(index == 0)
    def _():
        move(
            [
                (qkv_ref.at[1:3, :, cols(c)], low_s.at[i], [(low_s.at[i], low_refs[i])])
                for i, c in enumerate(lows)
            ]
        )

    if asks:

        @pl.when(index >= 2)
        def _():
            move(ask_steps())


def params(limit=VMEM_LIMIT):
    return pltpu.CompilerParams(vmem_limit_bytes=limit)


NONE = pl.CostEstimate(flops=1, bytes_accessed=1, transcendentals=0)
COVER = pl.CostEstimate(flops=int(2e10), bytes_accessed=int(8e7), transcendentals=0)
SMEM = pl.BlockSpec(memory_space=pltpu.SMEM)


def shape(dims, kind):
    return jax.ShapeDtypeStruct(dims, kind)


def full(array):
    return pl.BlockSpec(array.shape, lambda j: (0,) * array.ndim)


def se_mixer(qkv, tail, short, filt):
    rows, width = qkv.shape[1:]
    cols = 256
    return pl.pallas_call(
        se_kernel,
        grid=(width // cols,),
        in_specs=[
            pl.BlockSpec((3, rows, cols), lambda j: (0, 0, j)),
            pl.BlockSpec((tail.shape[0], cols), lambda j: (0, j)),
            pl.BlockSpec((3, 3, cols), lambda j: (0, 0, j)),
            pl.BlockSpec((filt.shape[0], cols), lambda j: (0, j)),
        ],
        out_specs=pl.BlockSpec((rows, cols), lambda j: (0, j)),
        out_shape=shape((rows, width), BF16),
        scratch_shapes=[
            pltpu.VMEM((8 + rows, cols), F32),
            pltpu.VMEM((16 + rows, cols), F32),
            pltpu.VMEM((16 + rows, cols), F32),
            pltpu.VMEM((8 + rows, cols), F32),
        ],
        compiler_params=params(),
        cost_estimate=NONE,
        name="se_mixer",
    )(qkv, tail, short, filt)


def raw_of(se_qkv, mr_qkv):
    rows, width = mr_qkv.shape[1:]
    last = rows // 16 - 1
    tail = pl.BlockSpec((3, 16, width), lambda j: (0, last, 0))
    return pl.pallas_call(
        raw_kernel,
        grid=(1,),
        in_specs=[tail, tail],
        out_specs=pl.BlockSpec((32, width), lambda j: (0, 0)),
        out_shape=shape((32, width), BF16),
        compiler_params=params(VMEM_EARLY),
        cost_estimate=NONE,
        name="raw_tail",
    )(se_qkv, mr_qkv)


def product_of(mr_qkv, short):
    rows, width = mr_qkv.shape[1:]
    cols = min(1024, width)
    half = rows // 2
    return pl.pallas_call(
        tail_kernel,
        grid=(width // cols,),
        in_specs=[
            pl.BlockSpec((1, half, cols), lambda j: (1, 1, j)),
            pl.BlockSpec((1, half, cols), lambda j: (2, 1, j)),
            pl.BlockSpec((3, 3, cols), lambda j: (0, 0, j)),
        ],
        out_specs=pl.BlockSpec((BLOCK, cols), lambda j: (0, j)),
        out_shape=shape((BLOCK, width), BF16),
        scratch_shapes=[pltpu.VMEM((half, cols), F32), pltpu.VMEM((half, cols), F32)],
        compiler_params=params(VMEM_EARLY),
        cost_estimate=COVER,
        name="product_tail",
    )(mr_qkv, mr_qkv, short)


def pack(index, qkv, lows, asks):
    rows, width = qkv.shape[1:]
    count = width // HD // PARTS
    part = count * HD
    anywhere = pl.BlockSpec(memory_space=pl.ANY)
    total = len(lows) + len(asks)
    out = pl.pallas_call(
        functools.partial(pack_kernel, lows, asks, part),
        in_specs=[SMEM, anywhere],
        out_specs=[anywhere] * total,
        out_shape=[shape((2, rows, part), BF16)] * len(lows)
        + [sent_shape(count, rows)] * len(asks),
        scratch_shapes=[
            pltpu.VMEM((max(len(lows), 1), 2, rows, part), BF16),
            pltpu.VMEM((max(len(asks), 1), rows, part), BF16),
            pltpu.SemaphoreType.DMA((2, len(lows) + len(asks) * count)),
        ],
        compiler_params=params(VMEM_EARLY),
        cost_estimate=NONE,
        name="pack",
    )(index, qkv)
    return out[: len(lows)], out[len(lows) :]


def mr_main(qkv, tail, short, filt, decay, fwd, inv):
    rows, width = qkv.shape[1:]
    cols = 512
    col = lambda j: (0, j)
    return pl.pallas_call(
        mr_main_kernel,
        grid=(width // cols,),
        in_specs=[
            pl.BlockSpec((3, rows, cols), lambda j: (0, 0, j)),
            pl.BlockSpec((tail.shape[0], cols), col),
            pl.BlockSpec((3, 3, cols), lambda j: (0, 0, j)),
            pl.BlockSpec((filt.shape[0], cols), col),
            pl.BlockSpec((1, cols), col),
            full(fwd),
            full(inv),
        ],
        out_specs=[
            pl.BlockSpec((rows, cols), col),
            pl.BlockSpec((WINDOW, cols), col),
            pl.BlockSpec((BLOCK, cols), col),
        ],
        out_shape=[
            shape((rows, width), BF16),
            shape((WINDOW, width), F32),
            shape((BLOCK, width), BF16),
        ],
        scratch_shapes=[pltpu.VMEM((8 + rows, cols), F32)] * 3 + [pltpu.VMEM((rows, cols), BF16)],
        compiler_params=params(),
        cost_estimate=NONE,
        name="mr_main",
    )(qkv, tail, short, filt, decay[None, :], fwd, inv)


def mr_head(index, low, high, lead, spec, qkv, tail, short, fwd, inv, part):
    rows, width = qkv.shape[1:]
    cols = 512
    col = lambda j: (0, j)
    return pl.pallas_call(
        mr_head_kernel,
        grid=(width // cols,),
        in_specs=[
            SMEM,
            pl.BlockSpec((BLOCK, cols), col),
            pl.BlockSpec((BLOCK, cols), col),
            pl.BlockSpec((BLOCK, cols), col),
            pl.BlockSpec((WINDOW, cols), col),
            pl.BlockSpec((1, BLOCK, cols), lambda j: (0, 0, j)),
            pl.BlockSpec((tail.shape[0], cols), col),
            pl.BlockSpec((3, 3, cols), lambda j: (0, 0, j)),
            full(fwd),
            full(inv),
            pl.BlockSpec(memory_space=pl.ANY),
        ],
        out_specs=pl.BlockSpec((BLOCK, cols), col),
        out_shape=shape((rows, width), BF16),
        scratch_shapes=[pltpu.VMEM((8 + BLOCK, cols), F32)],
        input_output_aliases={10: 0},
        compiler_params=params(),
        cost_estimate=NONE,
        name="mr_head",
    )(index, low, high, lead, spec, qkv, tail, short, fwd, inv, part)


def per_step(count):
    return 2 if count % 2 == 0 else 1


def sent_shape(count, rows):
    per = per_step(count)
    return shape((count // per, per * rows + STAT_ROWS, HD), BF16)


def head_spec(which, rows, per, offset):
    return pl.BlockSpec((1, rows, per * HD), lambda h: (which, 0, h + offset // per))


def unless_first(place):
    return lambda h, idx: jnp.where(idx[0] == 1, 0, h + place)


def local_attention(index, qkv):
    rows, width = qkv.shape[1:]
    heads = width // HD
    per = 4 if heads % 4 == 0 else 1
    at = unless_first(0)

    def part(which):
        return pl.BlockSpec((1, rows, per * HD), lambda h, idx: (which, 0, at(h, idx)))

    return pl.pallas_call(
        local_kernel,
        grid_spec=pltpu.PrefetchScalarGridSpec(
            num_scalar_prefetch=1,
            grid=(heads // per,),
            in_specs=[part(j) for j in range(3)],
            out_specs=[
                pl.BlockSpec((per, rows, HD), lambda h, idx: (at(h, idx), 0, 0)),
                pl.BlockSpec((per, 8, padded(rows)), lambda h, idx: (at(h, idx), 0, 0)),
            ],
        ),
        out_shape=[shape((heads, rows, HD), F32), shape((heads, 8, padded(rows)), F32)],
        compiler_params=params(),
        cost_estimate=NONE,
        name="local_attention",
    )(index, qkv, qkv, qkv)


def cross_attention(index, qkv, first, near, last, done, c):
    rows, width = qkv.shape[1:]
    count = width // HD // PARTS
    per = per_step(count)
    steps = count // per
    block = pl.BlockSpec((1, per * rows + STAT_ROWS, HD), lambda h: (h, 0, 0))
    has_ahead = c + 2 < PARTS

    def part(which, chunk):
        return pl.BlockSpec((1, rows, per * HD), lambda h: (which, 0, h + chunk * steps))

    specs = [SMEM] + [part(j, c) for j in range(3)]
    specs.append(pl.BlockSpec((2, rows, per * HD), lambda h: (0, 0, h)))
    operands = [index, qkv, qkv, qkv, first]
    if has_ahead:
        specs.append(part(0, c + 2))
        operands.append(qkv)
    operands += [near, last]
    specs += [block, block]
    aliases = {}
    if done is not None:
        aliases = {len(operands): 0}
        operands.append(done)
        specs.append(pl.BlockSpec(memory_space=pl.ANY))
    return pl.pallas_call(
        functools.partial(cross_kernel, has_ahead, done is not None),
        grid=(steps,),
        in_specs=specs,
        out_specs=[pl.BlockSpec((rows, per * HD), lambda h: (0, h + c * steps)), block, block],
        out_shape=[shape((rows, width), BF16)]
        + [sent_shape(count, rows)] * 2,
        input_output_aliases=aliases,
        compiler_params=params(),
        cost_estimate=COVER if c == 0 else NONE,
        name="cross_attention",
    )(*operands)


def merge_attention(index, local, stats, ups, fars, done, first):
    rows, width = done.shape
    count = width // HD // PARTS
    per = per_step(count)
    steps = count // per
    parts = len(ups)
    there = unless_first(first * steps)

    def payload(c):
        def place(h, idx):
            return (jnp.where(idx[0] < 2, 0, jnp.clip(h - c * steps, 0, steps - 1)), 0, 0)

        return pl.BlockSpec((1, per * rows + STAT_ROWS, HD), place)

    flat = pl.BlockSpec((rows, per * HD), lambda h, idx: (0, there(h, idx)))
    return pl.pallas_call(
        functools.partial(merge_kernel, steps, parts),
        grid_spec=pltpu.PrefetchScalarGridSpec(
            num_scalar_prefetch=1,
            grid=(steps * parts,),
            in_specs=[
                pl.BlockSpec((per, rows, HD), lambda h, idx: (there(h, idx), 0, 0)),
                pl.BlockSpec((per, 8, padded(rows)), lambda h, idx: (there(h, idx), 0, 0)),
            ]
            + [payload(c) for c in range(parts)] * 2
            + [flat],
            out_specs=flat,
        ),
        out_shape=shape((rows, width), BF16),
        input_output_aliases={3 + 2 * parts: 0},
        compiler_params=params(),
        cost_estimate=NONE,
        name="merge_attention",
    )(index, local, stats, *ups, *fars, done)


def gathered_attention(attn_qkv):
    rows, width = attn_qkv.shape[1:]
    heads = width // HD
    pairs = lax.all_gather(attn_qkv[1:], "seq", axis=1, tiled=True)
    count = pairs.shape[1]
    query = attn_qkv[0].reshape(rows, heads, HD)
    positions = lax.axis_index("seq") * rows + jnp.arange(rows)
    visible = (jnp.arange(count)[None, :] <= positions[:, None])[None]
    scores = jnp.einsum(
        "qhd,khd->hqk", query, pairs[0].reshape(count, heads, HD), preferred_element_type=F32
    ) / jnp.sqrt(F32(HD))
    scores = jnp.where(visible, scores, F32(-1e30))
    peak = jnp.max(scores, axis=2, keepdims=True)
    weights = jnp.where(visible, jnp.exp(scores - peak), F32(0.0))
    total = jnp.sum(weights, axis=2)
    mixed = jnp.einsum(
        "hqk,khd->qhd",
        weights.astype(BF16),
        pairs[1].reshape(count, heads, HD),
        preferred_element_type=F32,
    )
    return (mixed / total.T[:, :, None]).astype(BF16).reshape(rows, width)


def after(value, *needed):
    return lax.optimization_barrier((value,) + needed)[0]


def on_device(se_qkv, se_short, se_filter, mr_qkv, mr_short, mr_filter, mr_decay, attn_qkv):
    rows, width = se_qkv.shape[1:]
    spans = lax.axis_size("seq")
    fwd, inv = (jnp.asarray(m) for m in transforms())
    rising = [(s, s + 1) for s in range(spans - 1)]
    if spans == 4 and width % (PARTS * HD) == 0:
        return four_spans(
            se_qkv, se_short, se_filter, mr_qkv, mr_short, mr_filter, mr_decay, attn_qkv, fwd, inv
        )
    raw = lax.ppermute(raw_of(se_qkv, mr_qkv), "seq", rising)
    product = product_of(mr_qkv, mr_short)
    se_out = se_mixer(se_qkv, raw, se_short, se_filter)
    mr_part, spec, lead = mr_main(mr_qkv, raw, mr_short, mr_filter, mr_decay, fwd, inv)
    utail = lax.ppermute(product, "seq", rising)
    attn_out = gathered_attention(attn_qkv)
    index = lax.axis_index("seq").astype(jnp.int32).reshape(1)
    mr_out = mr_head(
        index, utail, utail, lead, spec, mr_qkv, raw, mr_short, fwd, inv, mr_part
    )
    return (se_out, mr_out, attn_out)


def four_spans(
    se_qkv, se_short, se_filter, mr_qkv, mr_short, mr_filter, mr_decay, attn_qkv, fwd, inv
):
    width = attn_qkv.shape[2]
    count = width // HD // PARTS
    send = lambda value, *pairs: lax.ppermute(value, "seq", list(pairs))
    index = lax.axis_index("seq").astype(jnp.int32).reshape(1)
    raw_own = raw_of(se_qkv, mr_qkv)
    raw = send(raw_own, (0, 1), (1, 2), (2, 3))
    a_in, ask_in = pack(index, after(attn_qkv, raw_own), [0], [0])
    a, b, d, up, far = ({} for _ in range(5))
    from_above = [(2, 1), (3, 2)]
    merging = [(1, 2), (2, 3)]
    b[0] = send(ask_in[0], (3, 1))
    d[0] = send(ask_in[0], *from_above)
    a[0] = send(a_in[0], (0, 1))
    product = product_of(after(mr_qkv, a_in[0], raw), mr_short)
    upper = send(product, (1, 2), (2, 3))
    later = pack(index, after(attn_qkv, product), [1, 2, 3], [1])
    a_in, ask_in = a_in + later[0], ask_in + later[1]
    se_out = se_mixer(after(se_qkv, a_in[1]), raw, se_short, se_filter)

    def cross(c, done, *needed):
        return cross_attention(index, attn_qkv, after(a[c], *needed), d[c], b[c], done, c)

    a[1] = send(a_in[1], (0, 1))
    b[1] = send(after(ask_in[1], b[0], d[0], se_out), (3, 1))
    d[1] = send(after(ask_in[1], b[0], d[0], se_out), *from_above)
    attn_out, up[0], far[0] = cross(0, None, se_out, a_in[1])
    local, stats = local_attention(index, after(attn_qkv, up[0]))
    b[2] = send(up[0], (3, 1), *merging)
    d[2] = send(far[0], (1, 3), *from_above)
    a[2] = send(after(a_in[2], a[1], up[0]), (0, 1))
    attn_out, up[1], far[1] = cross(1, attn_out, upper, stats)
    a[3] = send(after(a_in[3], up[1]), (0, 1))
    b[3] = send(up[1], (3, 1), *merging)
    d[3] = send(after(far[1], b[2], d[2]), (1, 3), *from_above)
    lower = send(after(product, a[2], up[1]), (0, 1))
    attn_out, up[2], far[2] = cross(2, attn_out)
    b[4] = send(up[2], *merging)
    d[4] = send(after(far[2], b[3]), (1, 3))
    attn_out, up[3], far[3] = cross(3, attn_out)
    b[5] = send(up[3], *merging)
    d[5] = send(far[3], (1, 3))
    mr_part, spec, lead = mr_main(
        after(mr_qkv, attn_out), raw, mr_short, mr_filter, mr_decay, fwd, inv
    )
    attn_out = merge_attention(
        index,
        after(local, lead),
        stats,
        [b[c + 2] for c in range(PARTS - 1)],
        [d[c + 2] for c in range(PARTS - 1)],
        attn_out,
        0,
    )
    mr_out = mr_head(index, lower, upper, lead, spec, mr_qkv, raw, mr_short, fwd, inv, mr_part)
    attn_out = merge_attention(
        index,
        after(local, mr_out),
        stats,
        [b[PARTS + 1]],
        [d[PARTS + 1]],
        attn_out,
        PARTS - 1,
    )
    return (se_out, mr_out, attn_out)


def solution(mesh):
    in_specs = (
        P(None, ("groups", "seq"), "chan"),
        P(None, None, "chan"),
        P(None, "chan"),
        P(None, ("groups", "seq"), "chan"),
        P(None, None, "chan"),
        P(None, "chan"),
        P("chan"),
        P(None, ("groups", "seq"), "chan"),
    )
    out_specs = (
        P(("groups", "seq"), "chan"),
        P(("groups", "seq"), "chan"),
        P(("groups", "seq"), "chan"),
    )
    return jax.shard_map(
        on_device, mesh=mesh, in_specs=in_specs, out_specs=out_specs, check_vma=False
    )
```
